128 devices in a mesh: row: 8 (over z, y_lo), col: 16 (over y_hi, x, core).
Axes of the slice: x: 4, y: 4 (y_hi: 2, y_lo: 2; y = y_hi * 2 + y_lo), z: 4, core: 2. Of those that a mesh axis runs over, the one named last changes fastest.
Arguments:
- tiles: bfloat16 [8, 16, 128, 128, 128], P('row', 'col'), may hold values from -2 to 2
- tile_src: int32 [8, 16, 128], P('row', 'col'), may hold values from 0 to 127
- tile_out: int32 [8, 16, 128], P('row', 'col'), may hold values from 0 to 255, as said below
- basis0: bfloat16 [262144, 256], P(('row', 'col')), may hold values from -40 to 40
Outputs:
- ortho_basis: float32 [262144, 256], P(('row', 'col'))
- gram_factor: float32 [256, 256], replicated
The draws below stay inside these ranges and needn't reach their ends.
Inputs may be any that keep to these rules, and one draw needn't show every extreme that they name: `tile_out`: tile t of a device writes into a block owned by col index t // 8 of the same row: its value lies in (t // 8) * 16 to that plus 16 - 1.
All inputs are finite; a program needn't handle non-finite values.
Results may differ from the reference program's by a relative error of at most 0.0032.
Values may be sent and summed in bfloat16 or wider, within the bound.
No kernel may reach another device: no remote copies, remote signals or barrier semaphores. Data moves between devices by JAX's collectives and lax.ppermute only.
A program may use at most 192 MiB of HBM per device.

```python
import math
import jax
import jax.numpy as jnp
from jax import lax

BLOCK = 128
BASIS = 256
BLOCKS_DEV = 16
ITERS = 1
PER_PEER = 8
TILE_DEV = 128
ROWS_DEV = 2048
ITEMS = 262144
N_ROW = 8
N_COL = 16


def draw_tiles(key, part):
    key = jax.random.fold_in(key, 5)
    fan_in = BLOCK * N_COL * PER_PEER // BLOCKS_DEV
    shape = (N_ROW, N_COL, TILE_DEV, BLOCK, BLOCK)
    row_pos = jnp.arange(N_ROW, dtype=jnp.float32) / (N_ROW - 1)
    values = jnp.clip(jax.random.normal(key, shape, jnp.float32), -4.0, 4.0)
    amplitude = 1.0 + row_pos
    drawn = values * amplitude[:, None, None, None, None] / math.sqrt(fan_in)
    return drawn.astype(jnp.bfloat16)


def draw_tile_out(key, part):
    key = jax.random.fold_in(key, 11)
    local_block = jax.random.randint(key, (N_ROW, N_COL, TILE_DEV), 0, BLOCKS_DEV)
    owner_base = jnp.arange(TILE_DEV) // PER_PEER * BLOCKS_DEV
    return (local_block + owner_base[None, None, :]).astype(jnp.int32)


def draw_basis0(key, part):
    key = jax.random.fold_in(key, 23)
    scale_key, value_key = jax.random.split(key, 2)
    row_scale = jnp.exp(jax.random.uniform(scale_key, (ITEMS, 1), jnp.float32, 0.0, math.log(10.0)))
    values = jnp.clip(jax.random.normal(value_key, (ITEMS, BASIS), jnp.float32), -4.0, 4.0)
    drawn = values * row_scale
    return drawn.astype(jnp.bfloat16)


def plant(array, key, smallest, high):
    shape = array.shape
    place = [jax.random.randint(jax.random.fold_in(key, axis), (), 0, shape[axis]) for axis in range(len(shape))]
    array = array.at[tuple(place)].set(smallest)
    longest = shape.index(max(shape))
    place[longest] = (place[longest] + 1) % shape[longest]
    return array.at[tuple(place)].set(high)


def setup_inputs(seed: int = 0) -> dict:
    key_of = jax.random.split(jax.random.key(seed), 5)
    return {
        "tiles": draw_tiles(jax.random.fold_in(key_of[4], 71), 0),
        "tile_src": plant(jax.random.randint(key_of[1], (N_ROW, N_COL, TILE_DEV), 0, N_ROW * BLOCKS_DEV), jax.random.fold_in(key_of[1], 1), 0, (N_ROW * BLOCKS_DEV) - 1).astype(jnp.int32),
        "tile_out": draw_tile_out(jax.random.fold_in(key_of[4], 71), 0),
        "basis0": draw_basis0(jax.random.fold_in(key_of[4], 71), 0),
    }


def reference(tiles, tile_src, tile_out, basis0):
    group_count = N_ROW * N_COL
    item_count = ROWS_DEV * group_count
    current = basis0
    orthonormal = jnp.zeros((item_count, BASIS), jnp.float32)
    factor = jnp.zeros((BASIS, BASIS), jnp.float32)
    for iteration in range(ITERS):
        blocks = current.reshape(N_ROW, N_COL, BLOCKS_DEV, BLOCK, BASIS)

        def add_device(device_flat, accum_sum):
            row_place = device_flat // N_COL
            col_place = device_flat % N_COL
            column = lax.dynamic_index_in_dim(blocks, col_place, 1, keepdims=False)
            column = column.reshape(N_ROW * BLOCKS_DEV, BLOCK, BASIS)
            tile_row = lax.dynamic_index_in_dim(tiles, row_place, 0, keepdims=False)
            tiles_here = lax.dynamic_index_in_dim(tile_row, col_place, 0, keepdims=False)
            src_row = lax.dynamic_index_in_dim(tile_src, row_place, 0, keepdims=False)
            src_here = lax.dynamic_index_in_dim(src_row, col_place, 0, keepdims=False).astype(jnp.int32)
            out_row = lax.dynamic_index_in_dim(tile_out, row_place, 0, keepdims=False)
            out_here = lax.dynamic_index_in_dim(out_row, col_place, 0, keepdims=False).astype(jnp.int32)
            sources = jnp.take(column, src_here, axis=0)
            products = jnp.einsum('tij,tjk->tik', tiles_here.astype(jnp.float32), sources.astype(jnp.float32))
            rounded = lax.optimization_barrier(products.astype(jnp.bfloat16))
            targets = (row_place * (N_COL * BLOCKS_DEV)).astype(jnp.int32) + out_here
            return accum_sum.at[targets].add(rounded.astype(jnp.float32))
        start_sum = jnp.zeros((group_count * BLOCKS_DEV, BLOCK, BASIS), jnp.float32)
        summed = lax.fori_loop(0, group_count, add_device, start_sum).reshape(item_count, BASIS)
        gram_total = jnp.dot(summed.T, summed, precision=lax.Precision.HIGHEST) / item_count
        factor = jnp.linalg.cholesky(gram_total)
        orthonormal = lax.linalg.triangular_solve(factor, summed, left_side=False, lower=True, transpose_a=True)
        current = orthonormal.astype(jnp.bfloat16)
    return (orthonormal, factor)
```

```python
import jax
import jax.numpy as jnp
from jax import lax
from jax.experimental import pallas as pl
from jax.experimental.pallas import tpu as pltpu
from jax.sharding import PartitionSpec as P

BLOCK = 128
BASIS = 256
BLOCKS_DEV = 16
PER_PEER = 8
TILE_DEV = 128
ROWS_DEV = 2048
N_ROW = 8
N_COL = 16
ITEMS = 262144
BOTH = ("row", "col")


def device(z, y, x, core):
    z, y, x = z % 4, y % 4, x % 4
    return (z * 2 + y % 2) * N_COL + (y // 2 * 4 + x) * 2 + core


def shifted(value, dz=0, dy=0, dx=0, dcore=0):
    pairs = [
        (device(z, y, x, c), device(z + dz, y + dy, x + dx, (c + dcore) % 2))
        for z in range(4)
        for y in range(4)
        for x in range(4)
        for c in range(2)
    ]
    return lax.ppermute(value, BOTH, pairs)


def row_shifted(value, dz, flip):
    pairs = [(z * 2 + y, (z + dz) % 4 * 2 + (y ^ flip)) for z in range(4) for y in range(2)]
    return lax.ppermute(value, "row", pairs)


def gather_column(own):
    half = ROWS_DEV // 2
    below = row_shifted(own, 1, 0)
    above = row_shifted(own, -1, 0)
    beside = row_shifted(own, 0, 1)
    across_a = row_shifted(below[:half], 1, 0)
    across_b = row_shifted(above[half:], -1, 0)
    beside_above = row_shifted(above, 0, 1)
    beside_below = row_shifted(beside, 1, 0)
    beside_across = row_shifted(beside_above, -1, 0)
    return own, above, across_a, across_b, below, beside, beside_above, beside_across, beside_below


def product_kernel(src, tiles, *refs):
    parts, out, column, sems = refs[:9], refs[9], refs[10], refs[11]

    @pl.when(pl.program_id(0) == 0)
    def _():
        start = 0
        copies = []
        for i, part in enumerate(parts):
            rows = part.shape[0]
            copies.append(pltpu.make_async_copy(part, column.at[pl.ds(start, rows)], sems.at[i]))
            start += rows
        for copy in copies:
            copy.start()
        for copy in copies:
            copy.wait()

    for q in range(PER_PEER):
        place = src[pl.program_id(0) * PER_PEER + q]
        source = column[pl.ds(pl.multiple_of(place * BLOCK, BLOCK), BLOCK), :]
        product = jnp.dot(tiles[q], source, preferred_element_type=jnp.float32)
        out[pl.ds(q * BLOCK, BLOCK), :] = product.astype(jnp.bfloat16)


def make_products(src, tiles, parts):
    return pl.pallas_call(
        product_kernel,
        out_shape=jax.ShapeDtypeStruct((TILE_DEV * BLOCK, BASIS), jnp.bfloat16),
        grid_spec=pltpu.PrefetchScalarGridSpec(
            num_scalar_prefetch=1,
            grid=(N_COL,),
            in_specs=[pl.BlockSpec((PER_PEER, BLOCK, BLOCK), lambda p, src: (p, 0, 0))]
            + [pl.BlockSpec(memory_space=pl.ANY)] * 9,
            out_specs=pl.BlockSpec((PER_PEER * BLOCK, BASIS), lambda p, src: (p, 0)),
            scratch_shapes=[
                pltpu.VMEM((N_ROW * ROWS_DEV, BASIS), jnp.bfloat16),
                pltpu.SemaphoreType.DMA((9,)),
            ],
        ),
        compiler_params=pltpu.CompilerParams(vmem_limit_bytes=40 * 1024 * 1024),
        name="products",
    )(src, tiles, *parts)


def sum_kernel(place, products, summed, gram):
    p = pl.program_id(0)

    @pl.when(p == 0)
    def _():
        summed[...] = jnp.zeros_like(summed)

    for q in range(PER_PEER):
        rows = pl.ds(pl.multiple_of(place[p * PER_PEER + q] * BLOCK, BLOCK), BLOCK)
        summed[rows, :] += products[pl.ds(q * BLOCK, BLOCK), :].astype(jnp.float32)

    @pl.when(p == N_COL - 1)
    def _():
        def contract(a, b):
            return lax.dot_general(
                a,
                b,
                (((0,), (0,)), ((), ())),
                precision=lax.Precision.HIGHEST,
                preferred_element_type=jnp.float32,
            )

        left, right = summed[:, :BLOCK], summed[:, BLOCK:]
        gram[0:BLOCK, :] = contract(left, left)
        gram[BLOCK : 2 * BLOCK, :] = contract(left, right)
        gram[2 * BLOCK :, :] = contract(right, right)


def sum_and_gram(place, products):
    return pl.pallas_call(
        sum_kernel,
        out_shape=(
            jax.ShapeDtypeStruct((ROWS_DEV, BASIS), jnp.float32),
            jax.ShapeDtypeStruct((3 * BLOCK, BLOCK), jnp.float32),
        ),
        grid_spec=pltpu.PrefetchScalarGridSpec(
            num_scalar_prefetch=1,
            grid=(N_COL,),
            in_specs=[pl.BlockSpec((PER_PEER * BLOCK, BASIS), lambda p, place: (p, 0))],
            out_specs=(
                pl.BlockSpec((ROWS_DEV, BASIS), lambda p, place: (0, 0)),
                pl.BlockSpec((3 * BLOCK, BLOCK), lambda p, place: (0, 0)),
            ),
        ),
        compiler_params=pltpu.CompilerParams(vmem_limit_bytes=40 * 1024 * 1024),
        name="sum_and_gram",
    )(place, products)


def reduce_everywhere(gram):
    col = lax.axis_index("col")
    core, x = col % 2, col // 2 % 4
    rows = gram.shape[0] // 8

    def pick(parts, i):
        return lax.dynamic_index_in_dim(parts, i % parts.shape[0], 0, keepdims=False)

    halves = gram.reshape(2, 4 * rows, -1)
    part = pick(halves, core) + shifted(pick(halves, 1 - core), dcore=1)
    part = part.reshape(4, rows, -1)
    part = pick(part, x) + sum(shifted(pick(part, x + d), dx=d) for d in (1, 2, 3))
    part = part + sum(shifted(part, dy=d) for d in (1, 2, 3))
    part = part + sum(shifted(part, dz=d) for d in (1, 2, 3))
    parts = jnp.stack([part] + [shifted(part, dx=-d) for d in (1, 2, 3)])
    mine = jnp.concatenate([pick(parts, k - x) for k in range(4)])
    other = shifted(mine, dcore=1)
    return jnp.where(core == 0, jnp.concatenate([mine, other]), jnp.concatenate([other, mine]))


def local(tiles, tile_src, tile_out, basis0):
    row = lax.axis_index("row")
    places = lax.all_gather(tile_out[0, 0].reshape(N_COL, PER_PEER), "col", axis=0)
    place = lax.dynamic_index_in_dim(places, lax.axis_index("col"), 1, keepdims=False)
    place = (place % BLOCKS_DEV).reshape(-1)
    src = tile_src[0, 0]
    group = src // BLOCKS_DEV
    distance = (group // 2 - row // 2) % 4 + 4 * ((group + row) % 2)
    src = distance * BLOCKS_DEV + src % BLOCKS_DEV

    parts = gather_column(basis0)
    products = make_products(src, tiles[0, 0], parts)
    products = lax.all_to_all(
        products.reshape(N_COL, PER_PEER * BLOCK, BASIS), "col", 0, 0, tiled=True
    )
    summed, gram = sum_and_gram(place, products.reshape(-1, BASIS))
    gram = reduce_everywhere(gram) / ITEMS
    upper = gram[BLOCK : 2 * BLOCK]
    gram_total = jnp.concatenate(
        [
            jnp.concatenate([gram[:BLOCK], upper], axis=1),
            jnp.concatenate([upper.T, gram[2 * BLOCK :]], axis=1),
        ]
    )
    factor = jnp.linalg.cholesky(gram_total)
    orthonormal = lax.linalg.triangular_solve(
        factor, summed, left_side=False, lower=True, transpose_a=True
    )
    return (orthonormal, factor)


def solution(mesh):
    in_specs = (
        P("row", "col", None, None, None),
        P("row", "col", None),
        P("row", "col", None),
        P(("row", "col"), None),
    )
    out_specs = (P(("row", "col"), None), P())
    return jax.shard_map(local, mesh=mesh, in_specs=in_specs, out_specs=out_specs, check_vma=False)
```

```python
import jax
import jax.numpy as jnp
from jax import lax
from jax.experimental import pallas as pl
from jax.experimental.pallas import tpu as pltpu
from jax.sharding import PartitionSpec as P

BLOCK = 128
BASIS = 256
BLOCKS_DEV = 16
PER_PEER = 8
TILE_DEV = 128
ROWS_DEV = 2048
N_ROW = 8
N_COL = 16
ITEMS = 262144
BOTH = ("row", "col")
CUTS = (688, 1376)
PARTS = 10
PANEL = 16
PIECE = 48
CHUNKS = 16
OUT_CHUNKS = 8


def device(z, y, x, core):
    z, y, x = z % 4, y % 4, x % 4
    return (z * 2 + y % 2) * N_COL + (y // 2 * 4 + x) * 2 + core


def shifted(value, dz=0, dy=0, dx=0, dcore=0):
    pairs = [
        (device(z, y, x, c), device(z + dz, y + dy, x + dx, (c + dcore) % 2))
        for z in range(4)
        for y in range(4)
        for x in range(4)
        for c in range(2)
    ]
    return lax.ppermute(value, BOTH, pairs)


def row_shifted(value, dz, flip):
    pairs = [(z * 2 + y, (z + dz) % 4 * 2 + (y ^ flip)) for z in range(4) for y in range(2)]
    return lax.ppermute(value, "row", pairs)


def together(*values):
    return lax.optimization_barrier(values)


def gather_column(own, place):
    below = row_shifted(own, 1, 0)
    above = row_shifted(own, -1, 0)
    beside = row_shifted(own, 0, 1)
    below, above, beside, place = together(below, above, beside, place)
    across = row_shifted(above, -1, 0)
    beside_above = row_shifted(above, 0, 1)
    beside_below = row_shifted(beside, 1, 0)
    place = lax.all_to_all(place.reshape(N_COL, PER_PEER), "col", 0, 0, tiled=True).reshape(-1)
    across, beside_above, beside_below, place = together(across, beside_above, beside_below, place)
    first, second = CUTS
    last = (
        row_shifted(beside_below[:first], 1, 0),
        row_shifted(beside_above[first:second], -1, 0),
        row_shifted(across[second:], 0, 1),
    )
    return (own, above, across, below, beside, beside_above, *last, beside_below), place


def split(value):
    high = value.astype(jnp.bfloat16)
    rest = value - high.astype(jnp.float32)
    middle = rest.astype(jnp.bfloat16)
    low = (rest - middle.astype(jnp.float32)).astype(jnp.bfloat16)
    return high, middle, low


def product_kernel(src, tiles_hbm, *refs):
    parts = refs[:PARTS]
    out_hbm, tiles, column, out, tile_sems, part_sems, out_sems = refs[PARTS:]
    loads = []
    start = 0
    for i, part in enumerate(parts):
        rows = part.shape[0]
        loads.append(pltpu.make_async_copy(part, column.at[pl.ds(start, rows)], part_sems.at[i]))
        start += rows
    share = TILE_DEV // CHUNKS
    tile_loads = []
    for g in range(CHUNKS):
        here = pl.ds(g * share, share)
        tile_loads.append(pltpu.make_async_copy(tiles_hbm.at[here], tiles.at[here], tile_sems.at[g]))
    for load in loads + tile_loads:
        load.start()
    for load in loads:
        load.wait()
    stores = []
    for g in range(CHUNKS):
        tile_loads[g].wait()

        @pl.loop(g * share, (g + 1) * share, unroll=8)
        def _(t):
            source = column[pl.ds(pl.multiple_of(src[t] * BLOCK, BLOCK), BLOCK), :]
            product = jnp.dot(tiles[t], source, preferred_element_type=jnp.float32)
            out[pl.ds(pl.multiple_of(t * BLOCK, BLOCK), BLOCK), :] = product.astype(jnp.bfloat16)

        here = pl.ds(g * share * BLOCK, share * BLOCK)
        store = pltpu.make_async_copy(out.at[here], out_hbm.at[here], out_sems.at[g])
        store.start()
        stores.append(store)
    for store in stores:
        store.wait()


def make_products(src, tiles, parts):
    return pl.pallas_call(
        product_kernel,
        out_shape=jax.ShapeDtypeStruct((TILE_DEV * BLOCK, BASIS), jnp.bfloat16),
        in_specs=[pl.BlockSpec(memory_space=pltpu.SMEM)]
        + [pl.BlockSpec(memory_space=pltpu.HBM)] * (1 + PARTS),
        out_specs=pl.BlockSpec(memory_space=pltpu.HBM),
        scratch_shapes=[
            pltpu.VMEM((TILE_DEV, BLOCK, BLOCK), jnp.bfloat16),
            pltpu.VMEM((N_ROW * ROWS_DEV, BASIS), jnp.bfloat16),
            pltpu.VMEM((TILE_DEV * BLOCK, BASIS), jnp.bfloat16),
            pltpu.SemaphoreType.DMA((CHUNKS,)),
            pltpu.SemaphoreType.DMA((PARTS,)),
            pltpu.SemaphoreType.DMA((CHUNKS,)),
        ],
        compiler_params=pltpu.CompilerParams(vmem_limit_bytes=48 * 1024 * 1024),
        name="products",
    )(src, tiles, *parts)


def sum_kernel(place, me, products_hbm, summed_hbm, gram, products, summed, packed, in_sems, out_sem):
    share = TILE_DEV // CHUNKS
    loads = []
    for g in range(CHUNKS):
        here = pl.ds(g * share * BLOCK, share * BLOCK)
        loads.append(pltpu.make_async_copy(products_hbm.at[here], products.at[here], in_sems.at[g]))
    for load in loads:
        load.start()
    summed[...] = jnp.zeros_like(summed)
    for g in range(CHUNKS):
        loads[g].wait()

        @pl.loop(g * share, (g + 1) * share, unroll=4)
        def _(t):
            rows = pl.ds(pl.multiple_of(place[t] * BLOCK, BLOCK), BLOCK)
            product = products[pl.ds(pl.multiple_of(t * BLOCK, BLOCK), BLOCK), :]
            summed[rows, :] += product.astype(jnp.float32)

    store = pltpu.make_async_copy(summed, summed_hbm, out_sem)
    store.start()

    def contract(a, b):
        return lax.dot_general(
            a, b, (((0,), (0,)), ((), ())), preferred_element_type=jnp.float32
        )

    high, middle, low = split(summed[...])
    mixed = contract(high, middle) + contract(high, low)
    total = contract(high, high) + contract(middle, middle) + mixed + mixed.T
    packed[:BLOCK, :] = total[:BLOCK, :BLOCK]
    packed[BLOCK : 2 * BLOCK, :] = total[:BLOCK, BLOCK:]
    packed[2 * BLOCK :, :] = total[BLOCK:, BLOCK:]
    for i, order in enumerate(piece_order(me)):
        gram[order] = packed[i * PIECE : (i + 1) * PIECE, :]
    store.wait()


def sum_and_gram(place, me, products):
    return pl.pallas_call(
        sum_kernel,
        out_shape=(
            jax.ShapeDtypeStruct((ROWS_DEV, BASIS), jnp.float32),
            jax.ShapeDtypeStruct((8, PIECE, BLOCK), jnp.float32),
        ),
        in_specs=[pl.BlockSpec(memory_space=pltpu.SMEM)] * 2
        + [pl.BlockSpec(memory_space=pltpu.HBM)],
        out_specs=(pl.BlockSpec(memory_space=pltpu.HBM), pl.BlockSpec(memory_space=pltpu.VMEM)),
        scratch_shapes=[
            pltpu.VMEM((TILE_DEV * BLOCK, BASIS), jnp.bfloat16),
            pltpu.VMEM((ROWS_DEV, BASIS), jnp.float32),
            pltpu.VMEM((3 * BLOCK, BLOCK), jnp.float32),
            pltpu.SemaphoreType.DMA((CHUNKS,)),
            pltpu.SemaphoreType.DMA,
        ],
        compiler_params=pltpu.CompilerParams(vmem_limit_bytes=48 * 1024 * 1024),
        name="sum_and_gram",
    )(place, me, products)


def reduce_everywhere(gram):
    part = gram[:4] + shifted(gram[4:], dcore=1)
    part = part[0] + sum(shifted(part[d], dx=d) for d in (1, 2, 3))
    part = part + sum(shifted(part, dy=d) for d in (1, 2, 3))
    part = part + sum(shifted(part, dz=d) for d in (1, 2, 3))
    mine = jnp.stack([part] + [shifted(part, dx=-d) for d in (1, 2, 3)])
    return mine, shifted(mine, dcore=1)


def piece_order(me):
    return [((i // 4) ^ me[0]) * 4 + ((i % 4 - me[1]) & 3) for i in range(8)]


def finish_kernel(me, mine, other, summed_hbm, ortho_hbm, factor, gram, work, summed, ortho, in_sem, out_sems):
    load = pltpu.make_async_copy(summed_hbm, summed, in_sem)
    load.start()
    for i, order in enumerate(piece_order(me)):
        here = pl.ds(i * PIECE, PIECE)

        @pl.when(order < 4)
        def _():
            gram[here, :] = mine[order & 3]

        @pl.when(order >= 4)
        def _():
            gram[here, :] = other[order & 3]

    row_id = lax.broadcasted_iota(jnp.int32, (BASIS, BASIS), 0)
    col_id = lax.broadcasted_iota(jnp.int32, (BASIS, BASIS), 1)
    work[:BLOCK, :BLOCK] = gram[:BLOCK, :] * (1.0 / ITEMS)
    work[:BLOCK, BLOCK:BASIS] = gram[BLOCK : 2 * BLOCK, :] * (1.0 / ITEMS)
    work[BLOCK:, :BLOCK] = jnp.zeros((BLOCK, BLOCK), jnp.float32)
    work[BLOCK:, BLOCK:BASIS] = gram[2 * BLOCK :, :] * (1.0 / ITEMS)
    work[:, BASIS:] = jnp.where(row_id == col_id, 1.0, 0.0)
    panel_row = lax.broadcasted_iota(jnp.int32, (PANEL, BLOCK), 0)
    for k in range(0, BASIS, PANEL):
        base = k // BLOCK * BLOCK
        window = pl.ds(base, 3 * BLOCK)
        panel = work[k : k + PANEL, window]
        strips = [panel[:, j * BLOCK : (j + 1) * BLOCK] for j in range(3)]
        columns = [
            jnp.broadcast_to(strips[0][:, k + i - base : k + i - base + 1], (PANEL, BLOCK))
            for i in range(PANEL)
        ]
        for i in range(PANEL):
            scale = lax.rsqrt(columns[i][i : i + 1, :])
            column = columns[i] * scale
            below = jnp.where(panel_row > i, column, 0.0)
            for j in range(3):
                pivot_row = strips[j][i : i + 1, :] * scale
                strips[j] = jnp.where(panel_row == i, pivot_row, strips[j] - below * pivot_row)
            for j in range(i + 1, PANEL):
                columns[j] = columns[j] - column * column[j : j + 1, :]
        panel = jnp.concatenate(strips, axis=1)
        work[k : k + PANEL, window] = panel
        after = k + PANEL
        if after < BASIS:
            high, middle, low = split(panel)
            left = jnp.concatenate([high, high, middle, middle, high, low], axis=0)
            right = jnp.concatenate([high, middle, high, middle, low, high], axis=0)
            update = lax.dot_general(
                left[:, : BASIS - base],
                right,
                (((0,), (0,)), ((), ())),
                preferred_element_type=jnp.float32,
            )
            work[after:, window] = work[after:, window] - update[after - base :, :]
    lower = row_id >= col_id
    factor[...] = jnp.where(lower, work[:, :BASIS].T, 0.0)
    inverse = jnp.where(lower, work[:, BASIS:], 0.0)
    load.wait()
    rows = ROWS_DEV // OUT_CHUNKS
    stores = []
    for i in range(OUT_CHUNKS):
        part = pl.ds(i * rows, rows)
        ortho[part, :] = lax.dot_general(
            summed[part, :],
            inverse,
            (((1,), (1,)), ((), ())),
            precision=lax.Precision.HIGHEST,
            preferred_element_type=jnp.float32,
        )
        store = pltpu.make_async_copy(ortho.at[part, :], ortho_hbm.at[part, :], out_sems.at[i])
        store.start()
        stores.append(store)
    for store in stores:
        store.wait()


def finish(me, mine, other, summed):
    return pl.pallas_call(
        finish_kernel,
        out_shape=(
            jax.ShapeDtypeStruct((ROWS_DEV, BASIS), jnp.float32),
            jax.ShapeDtypeStruct((BASIS, BASIS), jnp.float32),
        ),
        in_specs=[
            pl.BlockSpec(memory_space=pltpu.SMEM),
            pl.BlockSpec(memory_space=pltpu.VMEM),
            pl.BlockSpec(memory_space=pltpu.VMEM),
            pl.BlockSpec(memory_space=pl.ANY),
        ],
        out_specs=(pl.BlockSpec(memory_space=pl.ANY), pl.BlockSpec(memory_space=pltpu.VMEM)),
        scratch_shapes=[
            pltpu.VMEM((3 * BLOCK, BLOCK), jnp.float32),
            pltpu.VMEM((BASIS, 2 * BASIS), jnp.float32),
            pltpu.VMEM((ROWS_DEV, BASIS), jnp.float32),
            pltpu.VMEM((ROWS_DEV, BASIS), jnp.float32),
            pltpu.SemaphoreType.DMA,
            pltpu.SemaphoreType.DMA((OUT_CHUNKS,)),
        ],
        compiler_params=pltpu.CompilerParams(vmem_limit_bytes=40 * 1024 * 1024),
        name="finish",
    )(me, mine, other, summed)


def local(tiles, tile_src, tile_out, basis0):
    row = lax.axis_index("row").astype(jnp.int32)
    col = lax.axis_index("col").astype(jnp.int32)
    me = jnp.stack([col & 1, (col >> 1) & 3])
    src = tile_src[0, 0]
    group = src >> 4
    distance = (((group >> 1) - (row >> 1)) & 3) + 4 * ((group + row) & 1)
    src = distance * BLOCKS_DEV + (src & 15)

    parts, place = gather_column(basis0, tile_out[0, 0] & 15)
    products = make_products(src, tiles[0, 0], parts)
    products, place, me = together(products, place, me)
    products = lax.all_to_all(
        products.reshape(N_COL, PER_PEER * BLOCK, BASIS), "col", 0, 0, tiled=True
    )
    summed, gram = sum_and_gram(place, me, products.reshape(-1, BASIS))
    return finish(me, *reduce_everywhere(gram), summed)


def solution(mesh):
    in_specs = (
        P("row", "col", None, None, None),
        P("row", "col", None),
        P("row", "col", None),
        P(("row", "col"), None),
    )
    out_specs = (P(("row", "col"), None), P())
    return jax.shard_map(local, mesh=mesh, in_specs=in_specs, out_specs=out_specs, check_vma=False)
```

```python
import jax
import jax.numpy as jnp
from jax import lax
from jax.experimental import pallas as pl
from jax.experimental.pallas import tpu as pltpu
from jax.sharding import PartitionSpec as P

BLOCK = 128
BASIS = 256
BLOCKS_DEV = 16
PER_PEER = 8
TILE_DEV = 128
ROWS_DEV = 2048
N_ROW = 8
N_COL = 16
ITEMS = 262144
BOTH = ("row", "col")
PARTS = 14
PANEL = 32
PIECE = 48
CHUNKS = 16
OUT_CHUNKS = 8


def device(z, y, x, core):
    z, y, x = z % 4, y % 4, x % 4
    return (z * 2 + y % 2) * N_COL + (y // 2 * 4 + x) * 2 + core


def shifted(value, dz=0, dy=0, dx=0, dcore=0):
    pairs = [
        (device(z, y, x, c), device(z + dz, y + dy, x + dx, (c + dcore) % 2))
        for z in range(4)
        for y in range(4)
        for x in range(4)
        for c in range(2)
    ]
    return lax.ppermute(value, BOTH, pairs)


def row_shifted(value, dz, flip):
    pairs = [(z * 2 + y, (z + dz) % 4 * 2 + (y ^ flip)) for z in range(4) for y in range(2)]
    return lax.ppermute(value, "row", pairs)


def together(*values):
    return lax.optimization_barrier(values)


def gather_column(own, place):
    half = ROWS_DEV // 2
    below = row_shifted(own, 1, 0)
    above_a = row_shifted(own[:half], -1, 0)
    beside_a = row_shifted(own[:half], 0, 1)
    above_b = row_shifted(own[half:], -1, 0)
    beside_b = row_shifted(own[half:], 0, 1)
    beside_below_a = row_shifted(beside_a, 1, 0)
    beside_below_b = row_shifted(beside_b, 1, 0)
    across_a = row_shifted(above_a, -1, 0)
    across_b = row_shifted(above_b, -1, 0)
    below, above_a, above_b = together(below, above_a, above_b)
    beside_above_b = row_shifted(above_b, 0, 1)
    beside_above_a = row_shifted(above_a, 0, 1)
    beside_across_a = row_shifted(beside_below_a, 1, 0)
    beside_across_b = row_shifted(beside_above_b, -1, 0)
    across_a, across_b, beside_above_a, beside_below_b, place = together(
        across_a, across_b, beside_above_a, beside_below_b, place
    )
    place = lax.all_to_all(place.reshape(N_COL, 1, PER_PEER), "col", 0, 0, tiled=True)
    parts = (
        own, above_a, above_b, across_a, across_b, below, beside_a, beside_b,
        beside_above_a, beside_above_b, beside_across_a, beside_across_b,
        beside_below_a, beside_below_b,
    )
    return parts, place


def split(value):
    high = value.astype(jnp.bfloat16)
    rest = value - high.astype(jnp.float32)
    middle = rest.astype(jnp.bfloat16)
    low = (rest - middle.astype(jnp.float32)).astype(jnp.bfloat16)
    return high, middle, low


def product_kernel(src, tiles_hbm, *refs):
    parts = refs[:PARTS]
    out_hbm, tiles, column, out, tile_sems, part_sems, out_sems = refs[PARTS:]
    loads = []
    start = 0
    for i, part in enumerate(parts):
        rows = part.shape[0]
        loads.append(pltpu.make_async_copy(part, column.at[pl.ds(start, rows)], part_sems.at[i]))
        start += rows
    share = TILE_DEV // CHUNKS
    tile_loads = []
    for g in range(CHUNKS):
        here = pl.ds(g * share, share)
        tile_loads.append(pltpu.make_async_copy(tiles_hbm.at[here], tiles.at[here], tile_sems.at[g]))
    for load in loads + tile_loads:
        load.start()
    for load in loads:
        load.wait()
    stores = []
    for g in range(CHUNKS):
        tile_loads[g].wait()

        @pl.loop(g * share, (g + 1) * share, unroll=8)
        def _(t):
            source = column[pl.ds(pl.multiple_of(src[t] * BLOCK, BLOCK), BLOCK), :]
            product = jnp.dot(tiles[t], source, preferred_element_type=jnp.float32)
            out[pl.ds(pl.multiple_of(t * BLOCK, BLOCK), BLOCK), :] = product.astype(jnp.bfloat16)

        here = pl.ds(g * share * BLOCK, share * BLOCK)
        store = pltpu.make_async_copy(out.at[here], out_hbm.at[here], out_sems.at[g])
        store.start()
        stores.append(store)
    for store in stores:
        store.wait()


def make_products(src, tiles, parts):
    return pl.pallas_call(
        product_kernel,
        out_shape=jax.ShapeDtypeStruct((TILE_DEV * BLOCK, BASIS), jnp.bfloat16),
        in_specs=[pl.BlockSpec(memory_space=pltpu.SMEM)]
        + [pl.BlockSpec(memory_space=pltpu.HBM)] * (1 + PARTS),
        out_specs=pl.BlockSpec(memory_space=pltpu.HBM),
        scratch_shapes=[
            pltpu.VMEM((TILE_DEV, BLOCK, BLOCK), jnp.bfloat16),
            pltpu.VMEM((N_ROW * ROWS_DEV, BASIS), jnp.bfloat16),
            pltpu.VMEM((TILE_DEV * BLOCK, BASIS), jnp.bfloat16),
            pltpu.SemaphoreType.DMA((CHUNKS,)),
            pltpu.SemaphoreType.DMA((PARTS,)),
            pltpu.SemaphoreType.DMA((CHUNKS,)),
        ],
        compiler_params=pltpu.CompilerParams(vmem_limit_bytes=56 * 1024 * 1024),
        name="products",
    )(src, tiles, *parts)


def sum_kernel(place, me, products_hbm, summed_hbm, gram, products, summed, packed, in_sems, out_sem):
    share = TILE_DEV // CHUNKS
    loads = []
    for g in range(CHUNKS):
        here = pl.ds(g * share * BLOCK, share * BLOCK)
        loads.append(pltpu.make_async_copy(products_hbm.at[here], products.at[here], in_sems.at[g]))
    for load in loads:
        load.start()
    summed[...] = jnp.zeros_like(summed)
    for g in range(CHUNKS):
        loads[g].wait()

        @pl.loop(g * share, (g + 1) * share, unroll=4)
        def _(t):
            rows = pl.ds(pl.multiple_of(place[t >> 3, 0, t & 7] * BLOCK, BLOCK), BLOCK)
            product = products[pl.ds(pl.multiple_of(t * BLOCK, BLOCK), BLOCK), :]
            summed[rows, :] += product.astype(jnp.float32)

    store = pltpu.make_async_copy(summed, summed_hbm, out_sem)
    store.start()

    def contract(a, b):
        return lax.dot_general(
            a, b, (((0,), (0,)), ((), ())), preferred_element_type=jnp.float32
        )

    high, middle, low = split(summed[...])
    mixed = contract(high, middle) + contract(high, low)
    total = contract(high, high) + contract(middle, middle) + mixed + mixed.T
    packed[:BLOCK, :] = total[:BLOCK, :BLOCK]
    packed[BLOCK : 2 * BLOCK, :] = total[:BLOCK, BLOCK:]
    packed[2 * BLOCK :, :] = total[BLOCK:, BLOCK:]
    for i, order in enumerate(piece_order(me)):
        gram[order] = packed[i * PIECE : (i + 1) * PIECE, :]
    store.wait()


def sum_and_gram(place, me, products):
    return pl.pallas_call(
        sum_kernel,
        out_shape=(
            jax.ShapeDtypeStruct((ROWS_DEV, BASIS), jnp.float32),
            jax.ShapeDtypeStruct((8, PIECE, BLOCK), jnp.float32),
        ),
        in_specs=[pl.BlockSpec(memory_space=pltpu.SMEM)] * 2
        + [pl.BlockSpec(memory_space=pltpu.HBM)],
        out_specs=(pl.BlockSpec(memory_space=pltpu.HBM), pl.BlockSpec(memory_space=pltpu.VMEM)),
        scratch_shapes=[
            pltpu.VMEM((TILE_DEV * BLOCK, BASIS), jnp.bfloat16),
            pltpu.VMEM((ROWS_DEV, BASIS), jnp.float32),
            pltpu.VMEM((3 * BLOCK, BLOCK), jnp.float32),
            pltpu.SemaphoreType.DMA((CHUNKS,)),
            pltpu.SemaphoreType.DMA,
        ],
        compiler_params=pltpu.CompilerParams(vmem_limit_bytes=48 * 1024 * 1024),
        name="sum_and_gram",
    )(place, me, products)


def reduce_everywhere(gram):
    part = gram[:4] + shifted(gram[4:], dcore=1)
    part = part[0] + sum(shifted(part[d], dx=d) for d in (1, 2, 3))
    part = part + sum(shifted(part, dy=d) for d in (1, 2, 3))
    part = part + sum(shifted(part, dz=d) for d in (1, 2, 3))
    mine = jnp.stack([part] + [shifted(part, dx=-d) for d in (1, 2, 3)])
    return mine, shifted(mine, dcore=1)


def piece_order(me):
    return [((i // 4) ^ me[0]) * 4 + ((i % 4 - me[1]) & 3) for i in range(8)]


def finish_kernel(me, mine, other, summed_hbm, ortho_hbm, factor, gram, work, summed, ortho, in_sem, out_sems):
    load = pltpu.make_async_copy(summed_hbm, summed, in_sem)
    load.start()
    for i, order in enumerate(piece_order(me)):
        here = pl.ds(i * PIECE, PIECE)

        @pl.when(order < 4)
        def _():
            gram[here, :] = mine[order & 3]

        @pl.when(order >= 4)
        def _():
            gram[here, :] = other[order & 3]

    row_id = lax.broadcasted_iota(jnp.int32, (BASIS, BASIS), 0)
    col_id = lax.broadcasted_iota(jnp.int32, (BASIS, BASIS), 1)
    work[:BLOCK, :BLOCK] = gram[:BLOCK, :] * (1.0 / ITEMS)
    work[:BLOCK, BLOCK:BASIS] = gram[BLOCK : 2 * BLOCK, :] * (1.0 / ITEMS)
    work[BLOCK:, :BLOCK] = jnp.zeros((BLOCK, BLOCK), jnp.float32)
    work[BLOCK:, BLOCK:BASIS] = gram[2 * BLOCK :, :] * (1.0 / ITEMS)
    work[:, BASIS:] = jnp.where(row_id == col_id, 1.0, 0.0)
    panel_row = lax.broadcasted_iota(jnp.int32, (PANEL, BLOCK), 0)
    for k in range(0, BASIS, PANEL):
        base = k // BLOCK * BLOCK
        window = pl.ds(base, 3 * BLOCK)
        panel = work[k : k + PANEL, window]
        strips = [panel[:, j * BLOCK : (j + 1) * BLOCK] for j in range(3)]
        columns = [
            jnp.broadcast_to(strips[0][:, k + i - base : k + i - base + 1], (PANEL, BLOCK))
            for i in range(PANEL)
        ]
        for i in range(PANEL):
            scale = lax.rsqrt(columns[i][i : i + 1, :])
            column = columns[i] * scale
            below = jnp.where(panel_row > i, column, 0.0)
            for j in range(3):
                pivot_row = strips[j][i : i + 1, :] * scale
                strips[j] = jnp.where(panel_row == i, pivot_row, strips[j] - below * pivot_row)
            for j in range(i + 1, PANEL):
                columns[j] = columns[j] - column * column[j : j + 1, :]
        panel = jnp.concatenate(strips, axis=1)
        work[k : k + PANEL, window] = panel
        after = k + PANEL
        if after < BASIS:
            high, middle, low = split(panel)
            left = jnp.concatenate([high, high, middle, middle, high, low], axis=0)
            right = jnp.concatenate([high, middle, high, middle, low, high], axis=0)
            update = lax.dot_general(
                left[:, : BASIS - base],
                right,
                (((0,), (0,)), ((), ())),
                preferred_element_type=jnp.float32,
            )
            work[after:, window] = work[after:, window] - update[after - base :, :]
    lower = row_id >= col_id
    factor[...] = jnp.where(lower, work[:, :BASIS].T, 0.0)
    inverse = jnp.where(lower, work[:, BASIS:], 0.0)
    high, middle, _ = split(inverse)
    right = jnp.concatenate([high, middle, high], axis=1)
    load.wait()
    rows = ROWS_DEV // OUT_CHUNKS
    stores = []
    for i in range(OUT_CHUNKS):
        part = pl.ds(i * rows, rows)
        high, middle, _ = split(summed[part, :])
        ortho[part, :] = lax.dot_general(
            jnp.concatenate([high, high, middle], axis=1),
            right,
            (((1,), (1,)), ((), ())),
            preferred_element_type=jnp.float32,
        )
        store = pltpu.make_async_copy(ortho.at[part, :], ortho_hbm.at[part, :], out_sems.at[i])
        store.start()
        stores.append(store)
    for store in stores:
        store.wait()


def finish(me, mine, other, summed):
    return pl.pallas_call(
        finish_kernel,
        out_shape=(
            jax.ShapeDtypeStruct((ROWS_DEV, BASIS), jnp.float32),
            jax.ShapeDtypeStruct((BASIS, BASIS), jnp.float32),
        ),
        in_specs=[
            pl.BlockSpec(memory_space=pltpu.SMEM),
            pl.BlockSpec(memory_space=pltpu.VMEM),
            pl.BlockSpec(memory_space=pltpu.VMEM),
            pl.BlockSpec(memory_space=pl.ANY),
        ],
        out_specs=(pl.BlockSpec(memory_space=pl.ANY), pl.BlockSpec(memory_space=pltpu.VMEM)),
        scratch_shapes=[
            pltpu.VMEM((3 * BLOCK, BLOCK), jnp.float32),
            pltpu.VMEM((BASIS, 2 * BASIS), jnp.float32),
            pltpu.VMEM((ROWS_DEV, BASIS), jnp.float32),
            pltpu.VMEM((ROWS_DEV, BASIS), jnp.float32),
            pltpu.SemaphoreType.DMA,
            pltpu.SemaphoreType.DMA((OUT_CHUNKS,)),
        ],
        compiler_params=pltpu.CompilerParams(vmem_limit_bytes=40 * 1024 * 1024),
        name="finish",
    )(me, mine, other, summed)


def local(tiles, tile_src, tile_out, basis0):
    row = lax.axis_index("row").astype(jnp.int32)
    col = lax.axis_index("col").astype(jnp.int32)
    me = jnp.stack([col & 1, (col >> 1) & 3])
    src = tile_src[0, 0]
    group = src >> 4
    distance = (((group >> 1) - (row >> 1)) & 3) + 4 * ((group + row) & 1)
    src = distance * BLOCKS_DEV + (src & 15)

    parts, place = gather_column(basis0, tile_out[0, 0] & 15)
    products = make_products(src, tiles[0, 0], parts)
    products, place, me = together(products, place, me)
    products = lax.all_to_all(
        products.reshape(N_COL, PER_PEER * BLOCK, BASIS), "col", 0, 0, tiled=True
    )
    summed, gram = sum_and_gram(place, me, products.reshape(-1, BASIS))
    return finish(me, *reduce_everywhere(gram), summed)


def solution(mesh):
    in_specs = (
        P("row", "col", None, None, None),
        P("row", "col", None),
        P("row", "col", None),
        P(("row", "col"), None),
    )
    out_specs = (P(("row", "col"), None), P())
    return jax.shard_map(local, mesh=mesh, in_specs=in_specs, out_specs=out_specs, check_vma=False)
```

```python
import jax
import jax.numpy as jnp
from jax import lax
from jax.experimental import pallas as pl
from jax.experimental.pallas import tpu as pltpu
from jax.sharding import PartitionSpec as P

BLOCK = 128
BASIS = 256
BLOCKS_DEV = 16
PER_PEER = 8
TILE_DEV = 128
ROWS_DEV = 2048
N_ROW = 8
N_COL = 16
ITEMS = 262144
BOTH = ("row", "col")
PARTS = 14
LATE = (10, 11, 13, 12, 9, 8, 3, 4, 0)
PANEL = 32
PIECE = 48
CHUNKS = 16
OUT_CHUNKS = 8


def device(z, y, x, core):
    z, y, x = z % 4, y % 4, x % 4
    return (z * 2 + y % 2) * N_COL + (y // 2 * 4 + x) * 2 + core


def shifted(value, dz=0, dy=0, dx=0, dcore=0):
    pairs = [
        (device(z, y, x, c), device(z + dz, y + dy, x + dx, (c + dcore) % 2))
        for z in range(4)
        for y in range(4)
        for x in range(4)
        for c in range(2)
    ]
    return lax.ppermute(value, BOTH, pairs)


def row_shifted(value, dz, flip):
    pairs = [(z * 2 + y, (z + dz) % 4 * 2 + (y ^ flip)) for z in range(4) for y in range(2)]
    return lax.ppermute(value, "row", pairs)


def together(*values):
    return lax.optimization_barrier(values)


def gather_column(own, place):
    half = ROWS_DEV // 2
    below = row_shifted(own, 1, 0)
    above_a = row_shifted(own[:half], -1, 0)
    beside_a = row_shifted(own[:half], 0, 1)
    above_b = row_shifted(own[half:], -1, 0)
    beside_b = row_shifted(own[half:], 0, 1)
    beside_below_a = row_shifted(beside_a, 1, 0)
    beside_below_b = row_shifted(beside_b, 1, 0)
    across_a = row_shifted(above_a, -1, 0)
    across_b = row_shifted(above_b, -1, 0)
    below, above_a, above_b = together(below, above_a, above_b)
    beside_above_b = row_shifted(above_b, 0, 1)
    beside_above_a = row_shifted(above_a, 0, 1)
    beside_across_b = row_shifted(beside_below_b, 1, 0)
    beside_across_a = row_shifted(beside_above_a, -1, 0)
    across_a, across_b, beside_above_b, beside_below_a, place = together(
        across_a, across_b, beside_above_b, beside_below_a, place
    )
    place = lax.all_to_all(place.reshape(N_COL, 1, PER_PEER), "col", 0, 0, tiled=True)
    parts = (
        own, above_a, above_b, across_a, across_b, below, beside_a, beside_b,
        beside_above_a, beside_above_b, beside_across_a, beside_across_b,
        beside_below_a, beside_below_b,
    )
    return parts, place


def split(value):
    high = value.astype(jnp.bfloat16)
    rest = value - high.astype(jnp.float32)
    middle = rest.astype(jnp.bfloat16)
    low = (rest - middle.astype(jnp.float32)).astype(jnp.bfloat16)
    return high, middle, low


def product_kernel(src, tiles, *refs):
    parts = refs[:PARTS]
    out_hbm, column, out, part_sems, out_sems = refs[PARTS:]
    starts = [sum(part.shape[0] for part in parts[:i]) for i in range(PARTS)]
    places = [column.at[pl.ds(starts[i], parts[i].shape[0])] for i in range(PARTS)]
    loads = [
        pltpu.make_async_copy(parts[i], places[i], part_sems.at[k]) for k, i in enumerate(LATE)
    ]
    for load in loads:
        load.start()
    for i in range(PARTS):
        if i not in LATE:
            places[i][...] = parts[i][...]
    for load in loads:
        load.wait()
    share = TILE_DEV // CHUNKS
    stores = []
    for g in range(CHUNKS):

        @pl.loop(g * share, (g + 1) * share, unroll=8)
        def _(t):
            source = column[pl.ds(pl.multiple_of(src[t] * BLOCK, BLOCK), BLOCK), :]
            product = jnp.dot(tiles[t], source, preferred_element_type=jnp.float32)
            out[pl.ds(pl.multiple_of(t * BLOCK, BLOCK), BLOCK), :] = product.astype(jnp.bfloat16)

        here = pl.ds(g * share * BLOCK, share * BLOCK)
        store = pltpu.make_async_copy(out.at[here], out_hbm.at[here], out_sems.at[g])
        store.start()
        stores.append(store)
    for store in stores:
        store.wait()


def make_products(src, tiles, parts):
    return pl.pallas_call(
        product_kernel,
        out_shape=jax.ShapeDtypeStruct((TILE_DEV * BLOCK, BASIS), jnp.bfloat16),
        in_specs=[pl.BlockSpec(memory_space=pltpu.SMEM), pl.BlockSpec(memory_space=pltpu.VMEM)]
        + [
            pl.BlockSpec(memory_space=pltpu.HBM if i in LATE else pltpu.VMEM)
            for i in range(PARTS)
        ],
        out_specs=pl.BlockSpec(memory_space=pltpu.HBM),
        scratch_shapes=[
            pltpu.VMEM((N_ROW * ROWS_DEV, BASIS), jnp.bfloat16),
            pltpu.VMEM((TILE_DEV * BLOCK, BASIS), jnp.bfloat16),
            pltpu.SemaphoreType.DMA((len(LATE),)),
            pltpu.SemaphoreType.DMA((CHUNKS,)),
        ],
        compiler_params=pltpu.CompilerParams(vmem_limit_bytes=53 * 1024 * 1024),
        name="products",
    )(src, tiles, *parts)


def sum_kernel(place, me, products, summed_hbm, gram, summed, packed, out_sem):
    summed[...] = jnp.zeros_like(summed)

    @pl.loop(0, TILE_DEV, unroll=8)
    def _(t):
        rows = pl.ds(pl.multiple_of(place[t >> 3, 0, t & 7] * BLOCK, BLOCK), BLOCK)
        product = products[pl.ds(pl.multiple_of(t * BLOCK, BLOCK), BLOCK), :]
        summed[rows, :] += product.astype(jnp.float32)

    store = pltpu.make_async_copy(summed, summed_hbm, out_sem)
    store.start()

    def contract(a, b):
        return lax.dot_general(
            a, b, (((0,), (0,)), ((), ())), preferred_element_type=jnp.float32
        )

    high, middle, low = split(summed[...])
    mixed = contract(high, middle) + contract(high, low)
    total = contract(high, high) + contract(middle, middle) + mixed + mixed.T
    packed[:BLOCK, :] = total[:BLOCK, :BLOCK]
    packed[BLOCK : 2 * BLOCK, :] = total[:BLOCK, BLOCK:]
    packed[2 * BLOCK :, :] = total[BLOCK:, BLOCK:]
    for i, order in enumerate(piece_order(me)):
        gram[order] = packed[i * PIECE : (i + 1) * PIECE, :]
    store.wait()


def sum_and_gram(place, me, products):
    return pl.pallas_call(
        sum_kernel,
        out_shape=(
            jax.ShapeDtypeStruct((ROWS_DEV, BASIS), jnp.float32),
            jax.ShapeDtypeStruct((8, PIECE, BLOCK), jnp.float32),
        ),
        in_specs=[pl.BlockSpec(memory_space=pltpu.SMEM)] * 2
        + [pl.BlockSpec(memory_space=pltpu.VMEM)],
        out_specs=(pl.BlockSpec(memory_space=pltpu.HBM), pl.BlockSpec(memory_space=pltpu.VMEM)),
        scratch_shapes=[
            pltpu.VMEM((ROWS_DEV, BASIS), jnp.float32),
            pltpu.VMEM((3 * BLOCK, BLOCK), jnp.float32),
            pltpu.SemaphoreType.DMA,
        ],
        compiler_params=pltpu.CompilerParams(vmem_limit_bytes=32 * 1024 * 1024),
        name="sum_and_gram",
    )(place, me, products)


def reduce_everywhere(gram):
    part = gram[:4] + shifted(gram[4:], dcore=1)
    part = part[0] + sum(shifted(part[d], dx=d) for d in (1, 2, 3))
    part = part + sum(shifted(part, dy=d) for d in (1, 2, 3))
    part = part + sum(shifted(part, dz=d) for d in (1, 2, 3))
    mine = jnp.stack([part] + [shifted(part, dx=-d) for d in (1, 2, 3)])
    return mine, shifted(mine, dcore=1)


def piece_order(me):
    return [((i // 4) ^ me[0]) * 4 + ((i % 4 - me[1]) & 3) for i in range(8)]


def finish_kernel(me, mine, other, summed_hbm, ortho_hbm, factor, gram, work, summed, ortho, in_sem, out_sems):
    load = pltpu.make_async_copy(summed_hbm, summed, in_sem)
    load.start()
    for i, order in enumerate(piece_order(me)):
        here = pl.ds(i * PIECE, PIECE)

        @pl.when(order < 4)
        def _():
            gram[here, :] = mine[order & 3]

        @pl.when(order >= 4)
        def _():
            gram[here, :] = other[order & 3]

    row_id = lax.broadcasted_iota(jnp.int32, (BASIS, BASIS), 0)
    col_id = lax.broadcasted_iota(jnp.int32, (BASIS, BASIS), 1)
    work[:BLOCK, :BLOCK] = gram[:BLOCK, :] * (1.0 / ITEMS)
    work[:BLOCK, BLOCK:BASIS] = gram[BLOCK : 2 * BLOCK, :] * (1.0 / ITEMS)
    work[BLOCK:, :BLOCK] = jnp.zeros((BLOCK, BLOCK), jnp.float32)
    work[BLOCK:, BLOCK:BASIS] = gram[2 * BLOCK :, :] * (1.0 / ITEMS)
    work[:, BASIS:] = jnp.where(row_id == col_id, 1.0, 0.0)
    panel_row = lax.broadcasted_iota(jnp.int32, (PANEL, BLOCK), 0)
    for k in range(0, BASIS, PANEL):
        base = k // BLOCK * BLOCK
        window = pl.ds(base, 3 * BLOCK)
        panel = work[k : k + PANEL, window]
        strips = [panel[:, j * BLOCK : (j + 1) * BLOCK] for j in range(3)]
        columns = [
            jnp.broadcast_to(strips[0][:, k + i - base : k + i - base + 1], (PANEL, BLOCK))
            for i in range(PANEL)
        ]
        for i in range(PANEL):
            scale = lax.rsqrt(columns[i][i : i + 1, :])
            column = columns[i] * scale
            below = jnp.where(panel_row > i, column, 0.0)
            for j in range(3):
                pivot_row = strips[j][i : i + 1, :] * scale
                strips[j] = jnp.where(panel_row == i, pivot_row, strips[j] - below * pivot_row)
            for j in range(i + 1, PANEL):
                columns[j] = columns[j] - column * column[j : j + 1, :]
        panel = jnp.concatenate(strips, axis=1)
        work[k : k + PANEL, window] = panel
        after = k + PANEL
        if after < BASIS:
            high, middle, low = split(panel)
            left = jnp.concatenate([high, high, middle, middle, high, low], axis=0)
            right = jnp.concatenate([high, middle, high, middle, low, high], axis=0)
            update = lax.dot_general(
                left[:, : BASIS - base],
                right,
                (((0,), (0,)), ((), ())),
                preferred_element_type=jnp.float32,
            )
            work[after:, window] = work[after:, window] - update[after - base :, :]
    lower = row_id >= col_id
    factor[...] = jnp.where(lower, work[:, :BASIS].T, 0.0)
    inverse = jnp.where(lower, work[:, BASIS:], 0.0)
    high, middle, _ = split(inverse)
    right = jnp.concatenate([high, middle, high], axis=1)
    load.wait()
    rows = ROWS_DEV // OUT_CHUNKS
    stores = []
    for i in range(OUT_CHUNKS):
        part = pl.ds(i * rows, rows)
        high, middle, _ = split(summed[part, :])
        ortho[part, :] = lax.dot_general(
            jnp.concatenate([high, high, middle], axis=1),
            right,
            (((1,), (1,)), ((), ())),
            preferred_element_type=jnp.float32,
        )
        store = pltpu.make_async_copy(ortho.at[part, :], ortho_hbm.at[part, :], out_sems.at[i])
        store.start()
        stores.append(store)
    for store in stores:
        store.wait()


def finish(me, mine, other, summed):
    return pl.pallas_call(
        finish_kernel,
        out_shape=(
            jax.ShapeDtypeStruct((ROWS_DEV, BASIS), jnp.float32),
            jax.ShapeDtypeStruct((BASIS, BASIS), jnp.float32),
        ),
        in_specs=[
            pl.BlockSpec(memory_space=pltpu.SMEM),
            pl.BlockSpec(memory_space=pltpu.VMEM),
            pl.BlockSpec(memory_space=pltpu.VMEM),
            pl.BlockSpec(memory_space=pl.ANY),
        ],
        out_specs=(pl.BlockSpec(memory_space=pl.ANY), pl.BlockSpec(memory_space=pltpu.VMEM)),
        scratch_shapes=[
            pltpu.VMEM((3 * BLOCK, BLOCK), jnp.float32),
            pltpu.VMEM((BASIS, 2 * BASIS), jnp.float32),
            pltpu.VMEM((ROWS_DEV, BASIS), jnp.float32),
            pltpu.VMEM((ROWS_DEV, BASIS), jnp.float32),
            pltpu.SemaphoreType.DMA,
            pltpu.SemaphoreType.DMA((OUT_CHUNKS,)),
        ],
        compiler_params=pltpu.CompilerParams(vmem_limit_bytes=40 * 1024 * 1024),
        name="finish",
    )(me, mine, other, summed)


def local(tiles, tile_src, tile_out, basis0):
    row = lax.axis_index("row").astype(jnp.int32)
    col = lax.axis_index("col").astype(jnp.int32)
    me = jnp.stack([col & 1, (col >> 1) & 3])
    src = tile_src[0, 0]
    group = src >> 4
    distance = (((group >> 1) - (row >> 1)) & 3) + 4 * ((group + row) & 1)
    src = distance * BLOCKS_DEV + (src & 15)

    parts, place = gather_column(basis0, tile_out[0, 0] & 15)
    products = make_products(src, tiles[0, 0], parts)
    products, place, me = together(products, place, me)
    products = lax.all_to_all(
        products.reshape(N_COL, PER_PEER * BLOCK, BASIS), "col", 0, 0, tiled=True
    )
    summed, gram = sum_and_gram(place, me, products.reshape(-1, BASIS))
    return finish(me, *reduce_everywhere(gram), summed)


def solution(mesh):
    in_specs = (
        P("row", "col", None, None, None),
        P("row", "col", None),
        P("row", "col", None),
        P(("row", "col"), None),
    )
    out_specs = (P(("row", "col"), None), P())
    return jax.shard_map(local, mesh=mesh, in_specs=in_specs, out_specs=out_specs, check_vma=False)
```

```python
import jax
import jax.numpy as jnp
from jax import lax
from jax.experimental import pallas as pl
from jax.experimental.pallas import tpu as pltpu
from jax.sharding import PartitionSpec as P

BLOCK = 128
BASIS = 256
BLOCKS_DEV = 16
PER_PEER = 8
TILE_DEV = 128
ROWS_DEV = 2048
N_ROW = 8
N_COL = 16
ITEMS = 262144
BOTH = ("row", "col")
PARTS = 14
LATE = (10, 11, 13, 8, 4, 0)
PANEL = 32
SUB = 16
PIECE = 48
CHUNKS = 8
OUT_CHUNKS = 8


def device(z, y, x, core):
    z, y, x = z % 4, y % 4, x % 4
    return (z * 2 + y % 2) * N_COL + (y // 2 * 4 + x) * 2 + core


def shifted(value, dz=0, dy=0, dx=0, dcore=0):
    pairs = [
        (device(z, y, x, c), device(z + dz, y + dy, x + dx, (c + dcore) % 2))
        for z in range(4)
        for y in range(4)
        for x in range(4)
        for c in range(2)
    ]
    return lax.ppermute(value, BOTH, pairs)


def row_shifted(value, dz, flip):
    pairs = [(z * 2 + y, (z + dz) % 4 * 2 + (y ^ flip)) for z in range(4) for y in range(2)]
    return lax.ppermute(value, "row", pairs)


def together(*values):
    return lax.optimization_barrier(values)


def gather_column(own, place):
    half = ROWS_DEV // 2
    below = row_shifted(own, 1, 0)
    above_a = row_shifted(own[:half], -1, 0)
    beside_a = row_shifted(own[:half], 0, 1)
    above_b = row_shifted(own[half:], -1, 0)
    beside_b = row_shifted(own[half:], 0, 1)
    beside_below_a = row_shifted(beside_a, 1, 0)
    beside_below_b = row_shifted(beside_b, 1, 0)
    across_a = row_shifted(above_a, -1, 0)
    across_b = row_shifted(above_b, -1, 0)
    below, above_a, above_b = together(below, above_a, above_b)
    beside_above_b = row_shifted(above_b, 0, 1)
    beside_above_a = row_shifted(above_a, 0, 1)
    beside_across_b = row_shifted(beside_below_b, 1, 0)
    beside_across_a = row_shifted(beside_above_a, -1, 0)
    across_a, across_b, beside_above_b, beside_below_a, place = together(
        across_a, across_b, beside_above_b, beside_below_a, place
    )
    place = lax.all_to_all(place.reshape(N_COL, 1, PER_PEER), "col", 0, 0, tiled=True)
    parts = (
        own, above_a, above_b, across_a, across_b, below, beside_a, beside_b,
        beside_above_a, beside_above_b, beside_across_a, beside_across_b,
        beside_below_a, beside_below_b,
    )
    return parts, place


def split(value):
    high = value.astype(jnp.bfloat16)
    rest = value - high.astype(jnp.float32)
    middle = rest.astype(jnp.bfloat16)
    low = (rest - middle.astype(jnp.float32)).astype(jnp.bfloat16)
    return high, middle, low


def product_kernel(src, tiles, *refs):
    parts = refs[:PARTS]
    out_hbm, column, out, part_sems, out_sems = refs[PARTS:]
    starts = [sum(part.shape[0] for part in parts[:i]) for i in range(PARTS)]
    places = [column.at[pl.ds(starts[i], parts[i].shape[0])] for i in range(PARTS)]
    loads = [
        pltpu.make_async_copy(parts[i], places[i], part_sems.at[k]) for k, i in enumerate(LATE)
    ]
    for load in loads:
        load.start()
    for i in range(PARTS):
        if i not in LATE:
            places[i][...] = parts[i][...]
    for load in loads:
        load.wait()
    share = TILE_DEV // CHUNKS
    stores = []
    for g in range(CHUNKS):

        @pl.loop(g * share, (g + 1) * share, unroll=share)
        def _(t):
            source = column[pl.ds(pl.multiple_of(src[t] * BLOCK, BLOCK), BLOCK), :]
            product = jnp.dot(tiles[t], source, preferred_element_type=jnp.float32)
            out[pl.ds(pl.multiple_of(t * BLOCK, BLOCK), BLOCK), :] = product.astype(jnp.bfloat16)

        here = pl.ds(g * share * BLOCK, share * BLOCK)
        store = pltpu.make_async_copy(out.at[here], out_hbm.at[here], out_sems.at[g])
        store.start()
        stores.append(store)
    for store in stores:
        store.wait()


def make_products(src, tiles, parts):
    return pl.pallas_call(
        product_kernel,
        out_shape=jax.ShapeDtypeStruct((TILE_DEV * BLOCK, BASIS), jnp.bfloat16),
        in_specs=[pl.BlockSpec(memory_space=pltpu.SMEM), pl.BlockSpec(memory_space=pltpu.VMEM)]
        + [
            pl.BlockSpec(memory_space=pltpu.HBM if i in LATE else pltpu.VMEM)
            for i in range(PARTS)
        ],
        out_specs=pl.BlockSpec(memory_space=pltpu.HBM),
        scratch_shapes=[
            pltpu.VMEM((N_ROW * ROWS_DEV, BASIS), jnp.bfloat16),
            pltpu.VMEM((TILE_DEV * BLOCK, BASIS), jnp.bfloat16),
            pltpu.SemaphoreType.DMA((len(LATE),)),
            pltpu.SemaphoreType.DMA((CHUNKS,)),
        ],
        compiler_params=pltpu.CompilerParams(vmem_limit_bytes=51 * 1024 * 1024),
        name="products",
    )(src, tiles, *parts)


def sum_kernel(place, me, products, summed_hbm, gram, summed, packed, out_sem):
    summed[...] = jnp.zeros_like(summed)

    @pl.loop(0, TILE_DEV, unroll=8)
    def _(t):
        rows = pl.ds(pl.multiple_of(place[t >> 3, 0, t & 7] * BLOCK, BLOCK), BLOCK)
        product = products[pl.ds(pl.multiple_of(t * BLOCK, BLOCK), BLOCK), :]
        summed[rows, :] += product.astype(jnp.float32)

    store = pltpu.make_async_copy(summed, summed_hbm, out_sem)
    store.start()

    def contract(a, b):
        return lax.dot_general(
            a, b, (((0,), (0,)), ((), ())), preferred_element_type=jnp.float32
        )

    high, middle, low = split(summed[...])
    mixed = contract(high, middle) + contract(high, low)
    total = contract(high, high) + contract(middle, middle) + mixed + mixed.T
    packed[:BLOCK, :] = total[:BLOCK, :BLOCK]
    packed[BLOCK : 2 * BLOCK, :] = total[:BLOCK, BLOCK:]
    packed[2 * BLOCK :, :] = total[BLOCK:, BLOCK:]
    for i, order in enumerate(piece_order(me)):
        gram[order] = packed[i * PIECE : (i + 1) * PIECE, :]
    store.wait()


def sum_and_gram(place, me, products):
    return pl.pallas_call(
        sum_kernel,
        out_shape=(
            jax.ShapeDtypeStruct((ROWS_DEV, BASIS), jnp.float32),
            jax.ShapeDtypeStruct((8, PIECE, BLOCK), jnp.float32),
        ),
        in_specs=[pl.BlockSpec(memory_space=pltpu.SMEM)] * 2
        + [pl.BlockSpec(memory_space=pltpu.VMEM)],
        out_specs=(pl.BlockSpec(memory_space=pltpu.HBM), pl.BlockSpec(memory_space=pltpu.VMEM)),
        scratch_shapes=[
            pltpu.VMEM((ROWS_DEV, BASIS), jnp.float32),
            pltpu.VMEM((3 * BLOCK, BLOCK), jnp.float32),
            pltpu.SemaphoreType.DMA,
        ],
        compiler_params=pltpu.CompilerParams(vmem_limit_bytes=32 * 1024 * 1024),
        name="sum_and_gram",
    )(place, me, products)


def reduce_everywhere(gram):
    part = gram[:4] + shifted(gram[4:], dcore=1)
    part = part[0] + sum(shifted(part[d], dx=d) for d in (1, 2, 3))
    part = part + sum(shifted(part, dy=d) for d in (1, 2, 3))
    part = part + sum(shifted(part, dz=d) for d in (1, 2, 3))
    mine = jnp.stack([part] + [shifted(part, dx=-d) for d in (1, 2, 3)])
    return mine, shifted(mine, dcore=1)


def piece_order(me):
    return [((i // 4) ^ me[0]) * 4 + ((i % 4 - me[1]) & 3) for i in range(8)]


def finish_kernel(me, mine, other, summed_hbm, ortho_hbm, factor, gram, work, summed, ortho, in_sem, out_sems):
    load = pltpu.make_async_copy(summed_hbm, summed, in_sem)
    load.start()
    for i, order in enumerate(piece_order(me)):
        here = pl.ds(i * PIECE, PIECE)

        @pl.when(order < 4)
        def _():
            gram[here, :] = mine[order & 3]

        @pl.when(order >= 4)
        def _():
            gram[here, :] = other[order & 3]

    row_id = lax.broadcasted_iota(jnp.int32, (BASIS, BASIS), 0)
    col_id = lax.broadcasted_iota(jnp.int32, (BASIS, BASIS), 1)
    work[:BLOCK, :BLOCK] = gram[:BLOCK, :] * (1.0 / ITEMS)
    work[:BLOCK, BLOCK:BASIS] = gram[BLOCK : 2 * BLOCK, :] * (1.0 / ITEMS)
    work[BLOCK:, :BLOCK] = jnp.zeros((BLOCK, BLOCK), jnp.float32)
    work[BLOCK:, BLOCK:BASIS] = gram[2 * BLOCK :, :] * (1.0 / ITEMS)
    work[:, BASIS:] = jnp.where(row_id == col_id, 1.0, 0.0)
    sub_row = lax.broadcasted_iota(jnp.int32, (8, BLOCK), 0)
    groups = PANEL // 8
    lower = row_id >= col_id
    for k in range(0, BASIS, PANEL):
        base = k // BLOCK * BLOCK
        window = pl.ds(base, 3 * BLOCK)
        strips = [
            [work[k + 8 * g : k + 8 * g + 8, pl.ds(base + BLOCK * j, BLOCK)] for j in range(3)]
            for g in range(groups)
        ]
        for begin in range(0, PANEL, SUB):
            columns = {
                (i, g): jnp.broadcast_to(
                    strips[g][0][:, k + i - base : k + i - base + 1], (8, BLOCK)
                )
                for i in range(begin, begin + SUB)
                for g in range(begin // 8, groups)
            }
            for i in range(begin, begin + SUB):
                own, at = i // 8, i % 8
                scale = lax.rsqrt(columns[i, own][at : at + 1, :])
                column = {g: columns[i, g] * scale for g in range(own, groups)}
                for q in range(i + 1, begin + SUB):
                    near = column[q // 8][q % 8 : q % 8 + 1, :]
                    for g in range(own, groups):
                        columns[q, g] = columns[q, g] - column[g] * near
                below = jnp.where(sub_row > at, column[own], 0.0)
                for j in range(3):
                    pivot_row = strips[own][j][at : at + 1, :] * scale
                    strips[own][j] = jnp.where(
                        sub_row == at, pivot_row, strips[own][j] - below * pivot_row
                    )
                    for g in range(own + 1, groups):
                        strips[g][j] = strips[g][j] - column[g] * pivot_row
        panel = jnp.concatenate([jnp.concatenate(strip, axis=1) for strip in strips], axis=0)
        work[k : k + PANEL, window] = panel
        after = k + PANEL
        if after < BASIS:
            high, middle, low = split(panel)
            left = jnp.concatenate([high, high, middle, middle, high, low], axis=0)
            right = jnp.concatenate([high, middle, high, middle, low, high], axis=0)
            update = lax.dot_general(
                left[:, : BASIS - base],
                right,
                (((0,), (0,)), ((), ())),
                preferred_element_type=jnp.float32,
            )
            work[after:, window] = work[after:, window] - update[after - base :, :]
    factor[...] = jnp.where(lower, work[:, :BASIS].T, 0.0)
    inverse = jnp.where(lower, work[:, BASIS:], 0.0)
    high, middle, _ = split(inverse)
    right = jnp.concatenate([high, middle, high], axis=1)
    load.wait()
    rows = ROWS_DEV // OUT_CHUNKS
    stores = []
    for i in range(OUT_CHUNKS):
        part = pl.ds(i * rows, rows)
        high, middle, _ = split(summed[part, :])
        ortho[part, :] = lax.dot_general(
            jnp.concatenate([high, high, middle], axis=1),
            right,
            (((1,), (1,)), ((), ())),
            preferred_element_type=jnp.float32,
        )
        store = pltpu.make_async_copy(ortho.at[part, :], ortho_hbm.at[part, :], out_sems.at[i])
        store.start()
        stores.append(store)
    for store in stores:
        store.wait()


def finish(me, mine, other, summed):
    return pl.pallas_call(
        finish_kernel,
        out_shape=(
            jax.ShapeDtypeStruct((ROWS_DEV, BASIS), jnp.float32),
            jax.ShapeDtypeStruct((BASIS, BASIS), jnp.float32),
        ),
        in_specs=[
            pl.BlockSpec(memory_space=pltpu.SMEM),
            pl.BlockSpec(memory_space=pltpu.VMEM),
            pl.BlockSpec(memory_space=pltpu.VMEM),
            pl.BlockSpec(memory_space=pl.ANY),
        ],
        out_specs=(pl.BlockSpec(memory_space=pl.ANY), pl.BlockSpec(memory_space=pltpu.VMEM)),
        scratch_shapes=[
            pltpu.VMEM((3 * BLOCK, BLOCK), jnp.float32),
            pltpu.VMEM((BASIS, 2 * BASIS), jnp.float32),
            pltpu.VMEM((ROWS_DEV, BASIS), jnp.float32),
            pltpu.VMEM((ROWS_DEV, BASIS), jnp.float32),
            pltpu.SemaphoreType.DMA,
            pltpu.SemaphoreType.DMA((OUT_CHUNKS,)),
        ],
        compiler_params=pltpu.CompilerParams(vmem_limit_bytes=40 * 1024 * 1024),
        name="finish",
    )(me, mine, other, summed)


def local(tiles, tile_src, tile_out, basis0):
    row = lax.axis_index("row").astype(jnp.int32)
    col = lax.axis_index("col").astype(jnp.int32)
    me = jnp.stack([col & 1, (col >> 1) & 3])
    src = tile_src[0, 0]
    group = src >> 4
    distance = (((group >> 1) - (row >> 1)) & 3) + 4 * ((group + row) & 1)
    src = distance * BLOCKS_DEV + (src & 15)

    parts, place = gather_column(basis0, tile_out[0, 0] & 15)
    products = make_products(src, tiles[0, 0], parts)
    products, place, me = together(products, place, me)
    products = lax.all_to_all(
        products.reshape(N_COL, PER_PEER * BLOCK, BASIS), "col", 0, 0, tiled=True
    )
    summed, gram = sum_and_gram(place, me, products.reshape(-1, BASIS))
    return finish(me, *reduce_everywhere(gram), summed)


def solution(mesh):
    in_specs = (
        P("row", "col", None, None, None),
        P("row", "col", None),
        P("row", "col", None),
        P(("row", "col"), None),
    )
    out_specs = (P(("row", "col"), None), P())
    return jax.shard_map(local, mesh=mesh, in_specs=in_specs, out_specs=out_specs, check_vma=False)
```

```python
import jax
import jax.numpy as jnp
from jax import lax
from jax.experimental import pallas as pl
from jax.experimental.pallas import tpu as pltpu
from jax.sharding import PartitionSpec as P

BLOCK = 128
BASIS = 256
BLOCKS_DEV = 16
PER_PEER = 8
TILE_DEV = 128
ROWS_DEV = 2048
N_ROW = 8
N_COL = 16
ITEMS = 262144
BOTH = ("row", "col")
PARTS = 14
LATE = (10, 11, 13, 8, 4, 0)
PANEL = 32
SUB = 16
PIECE = 192
CHUNKS = 8
OUT_CHUNKS = 8


def device(z, y, x, core):
    z, y, x = z % 4, y % 4, x % 4
    return (z * 2 + y % 2) * N_COL + (y // 2 * 4 + x) * 2 + core


def shifted(value, dz=0, dy=0, dx=0, dcore=0):
    pairs = [
        (device(z, y, x, c), device(z + dz, y + dy, x + dx, (c + dcore) % 2))
        for z in range(4)
        for y in range(4)
        for x in range(4)
        for c in range(2)
    ]
    return lax.ppermute(value, BOTH, pairs)


def row_shifted(value, dz, flip):
    pairs = [(z * 2 + y, (z + dz) % 4 * 2 + (y ^ flip)) for z in range(4) for y in range(2)]
    return lax.ppermute(value, "row", pairs)


def together(*values):
    return lax.optimization_barrier(values)


def gather_column(own, place):
    half = ROWS_DEV // 2
    below = row_shifted(own, 1, 0)
    above_a = row_shifted(own[:half], -1, 0)
    beside_a = row_shifted(own[:half], 0, 1)
    above_b = row_shifted(own[half:], -1, 0)
    beside_b = row_shifted(own[half:], 0, 1)
    beside_below_a = row_shifted(beside_a, 1, 0)
    beside_below_b = row_shifted(beside_b, 1, 0)
    across_a = row_shifted(above_a, -1, 0)
    across_b = row_shifted(above_b, -1, 0)
    below, above_a, above_b = together(below, above_a, above_b)
    beside_above_b = row_shifted(above_b, 0, 1)
    beside_above_a = row_shifted(above_a, 0, 1)
    beside_across_b = row_shifted(beside_below_b, 1, 0)
    beside_across_a = row_shifted(beside_above_a, -1, 0)
    across_a, across_b, beside_above_b, beside_below_a, place = together(
        across_a, across_b, beside_above_b, beside_below_a, place
    )
    place = lax.all_to_all(place.reshape(N_COL, 1, PER_PEER), "col", 0, 0, tiled=True)
    parts = (
        own, above_a, above_b, across_a, across_b, below, beside_a, beside_b,
        beside_above_a, beside_above_b, beside_across_a, beside_across_b,
        beside_below_a, beside_below_b,
    )
    return parts, place


def split(value):
    high = value.astype(jnp.bfloat16)
    rest = value - high.astype(jnp.float32)
    middle = rest.astype(jnp.bfloat16)
    low = (rest - middle.astype(jnp.float32)).astype(jnp.bfloat16)
    return high, middle, low


def product_kernel(src, tiles, *refs):
    parts = refs[:PARTS]
    out_hbm, column, out, part_sems, out_sems = refs[PARTS:]
    starts = [sum(part.shape[0] for part in parts[:i]) for i in range(PARTS)]
    places = [column.at[pl.ds(starts[i], parts[i].shape[0])] for i in range(PARTS)]
    loads = [
        pltpu.make_async_copy(parts[i], places[i], part_sems.at[k]) for k, i in enumerate(LATE)
    ]
    for load in loads:
        load.start()
    for i in range(PARTS):
        if i not in LATE:
            places[i][...] = parts[i][...]
    for load in loads:
        load.wait()
    share = TILE_DEV // CHUNKS
    stores = []
    for g in range(CHUNKS):

        @pl.loop(g * share, (g + 1) * share, unroll=share)
        def _(t):
            source = column[pl.ds(pl.multiple_of(src[t] * BLOCK, BLOCK), BLOCK), :]
            product = jnp.dot(tiles[t], source, preferred_element_type=jnp.float32)
            out[pl.ds(pl.multiple_of(t * BLOCK, BLOCK), BLOCK), :] = product.astype(jnp.bfloat16)

        here = pl.ds(g * share * BLOCK, share * BLOCK)
        store = pltpu.make_async_copy(out.at[here], out_hbm.at[here], out_sems.at[g])
        store.start()
        stores.append(store)
    for store in stores:
        store.wait()


def make_products(src, tiles, parts):
    return pl.pallas_call(
        product_kernel,
        out_shape=jax.ShapeDtypeStruct((TILE_DEV * BLOCK, BASIS), jnp.bfloat16),
        in_specs=[pl.BlockSpec(memory_space=pltpu.SMEM), pl.BlockSpec(memory_space=pltpu.VMEM)]
        + [
            pl.BlockSpec(memory_space=pltpu.HBM if i in LATE else pltpu.VMEM)
            for i in range(PARTS)
        ],
        out_specs=pl.BlockSpec(memory_space=pltpu.HBM),
        scratch_shapes=[
            pltpu.VMEM((N_ROW * ROWS_DEV, BASIS), jnp.bfloat16),
            pltpu.VMEM((TILE_DEV * BLOCK, BASIS), jnp.bfloat16),
            pltpu.SemaphoreType.DMA((len(LATE),)),
            pltpu.SemaphoreType.DMA((CHUNKS,)),
        ],
        compiler_params=pltpu.CompilerParams(vmem_limit_bytes=51 * 1024 * 1024),
        name="products",
    )(src, tiles, *parts)


def sum_kernel(place, me, products, summed_hbm, gram, summed, packed, out_sem):
    summed[...] = jnp.zeros_like(summed)

    @pl.loop(0, TILE_DEV, unroll=8)
    def _(t):
        rows = pl.ds(pl.multiple_of(place[t >> 3, 0, t & 7] * BLOCK, BLOCK), BLOCK)
        product = products[pl.ds(pl.multiple_of(t * BLOCK, BLOCK), BLOCK), :]
        summed[rows, :] += product.astype(jnp.float32)

    store = pltpu.make_async_copy(summed, summed_hbm, out_sem)
    store.start()

    def contract(a, b):
        return lax.dot_general(
            a, b, (((0,), (0,)), ((), ())), preferred_element_type=jnp.float32
        )

    high, middle, low = split(summed[...])
    mixed = contract(high, middle) + contract(high, low)
    total = contract(high, high) + contract(middle, middle) + mixed + mixed.T
    packed[:BLOCK, :] = total[:BLOCK, :BLOCK]
    packed[BLOCK : 2 * BLOCK, :] = total[:BLOCK, BLOCK:]
    packed[2 * BLOCK :, :] = total[BLOCK:, BLOCK:]
    for i in range(2):
        gram[i ^ me[0]] = packed[i * PIECE : (i + 1) * PIECE, :]
    store.wait()


def sum_and_gram(place, me, products):
    return pl.pallas_call(
        sum_kernel,
        out_shape=(
            jax.ShapeDtypeStruct((ROWS_DEV, BASIS), jnp.float32),
            jax.ShapeDtypeStruct((2, PIECE, BLOCK), jnp.float32),
        ),
        in_specs=[pl.BlockSpec(memory_space=pltpu.SMEM)] * 2
        + [pl.BlockSpec(memory_space=pltpu.VMEM)],
        out_specs=(pl.BlockSpec(memory_space=pltpu.HBM), pl.BlockSpec(memory_space=pltpu.VMEM)),
        scratch_shapes=[
            pltpu.VMEM((ROWS_DEV, BASIS), jnp.float32),
            pltpu.VMEM((3 * BLOCK, BLOCK), jnp.float32),
            pltpu.SemaphoreType.DMA,
        ],
        compiler_params=pltpu.CompilerParams(vmem_limit_bytes=32 * 1024 * 1024),
        name="sum_and_gram",
    )(place, me, products)


def reduce_everywhere(gram):
    mine = gram[0] + shifted(gram[1], dcore=1)
    mine = mine + sum(shifted(mine, dx=d) for d in (1, 2, 3))
    mine = mine + sum(shifted(mine, dy=d) for d in (1, 2, 3))
    mine = mine + sum(shifted(mine, dz=d) for d in (1, 2, 3))
    return mine, shifted(mine, dcore=1)


def finish_kernel(me, mine, other, summed_hbm, ortho_hbm, factor, gram, work, summed, ortho, in_sem, out_sems):
    load = pltpu.make_async_copy(summed_hbm, summed, in_sem)
    load.start()
    gram[pl.ds(pl.multiple_of(me[0] * PIECE, 8), PIECE), :] = mine[...]
    gram[pl.ds(pl.multiple_of((1 - me[0]) * PIECE, 8), PIECE), :] = other[...]
    row_id = lax.broadcasted_iota(jnp.int32, (BASIS, BASIS), 0)
    col_id = lax.broadcasted_iota(jnp.int32, (BASIS, BASIS), 1)
    work[:BLOCK, :BLOCK] = gram[:BLOCK, :] * (1.0 / ITEMS)
    work[:BLOCK, BLOCK:BASIS] = gram[BLOCK : 2 * BLOCK, :] * (1.0 / ITEMS)
    work[BLOCK:, :BLOCK] = jnp.zeros((BLOCK, BLOCK), jnp.float32)
    work[BLOCK:, BLOCK:BASIS] = gram[2 * BLOCK :, :] * (1.0 / ITEMS)
    work[:, BASIS:] = jnp.where(row_id == col_id, 1.0, 0.0)
    sub_row = lax.broadcasted_iota(jnp.int32, (8, BLOCK), 0)
    groups = PANEL // 8
    lower = row_id >= col_id
    for k in range(0, BASIS, PANEL):
        base = k // BLOCK * BLOCK
        window = pl.ds(base, 3 * BLOCK)
        strips = [
            [work[k + 8 * g : k + 8 * g + 8, pl.ds(base + BLOCK * j, BLOCK)] for j in range(3)]
            for g in range(groups)
        ]
        for begin in range(0, PANEL, SUB):
            columns = {
                (i, g): jnp.broadcast_to(
                    strips[g][0][:, k + i - base : k + i - base + 1], (8, BLOCK)
                )
                for i in range(begin, begin + SUB)
                for g in range(begin // 8, groups)
            }
            for i in range(begin, begin + SUB):
                own, at = i // 8, i % 8
                scale = lax.rsqrt(columns[i, own][at : at + 1, :])
                column = {g: columns[i, g] * scale for g in range(own, groups)}
                for q in range(i + 1, begin + SUB):
                    near = column[q // 8][q % 8 : q % 8 + 1, :]
                    for g in range(own, groups):
                        columns[q, g] = columns[q, g] - column[g] * near
                below = jnp.where(sub_row > at, column[own], 0.0)
                for j in range(3):
                    pivot_row = strips[own][j][at : at + 1, :] * scale
                    strips[own][j] = jnp.where(
                        sub_row == at, pivot_row, strips[own][j] - below * pivot_row
                    )
                    for g in range(own + 1, groups):
                        strips[g][j] = strips[g][j] - column[g] * pivot_row
        panel = jnp.concatenate([jnp.concatenate(strip, axis=1) for strip in strips], axis=0)
        work[k : k + PANEL, window] = panel
        after = k + PANEL
        if after < BASIS:
            high, middle, low = split(panel)
            left = jnp.concatenate([high, high, middle, middle, high, low], axis=0)
            right = jnp.concatenate([high, middle, high, middle, low, high], axis=0)
            update = lax.dot_general(
                left[:, : BASIS - base],
                right,
                (((0,), (0,)), ((), ())),
                preferred_element_type=jnp.float32,
            )
            work[after:, window] = work[after:, window] - update[after - base :, :]
    factor[...] = jnp.where(lower, work[:, :BASIS].T, 0.0)
    inverse = jnp.where(lower, work[:, BASIS:], 0.0)
    high, middle, _ = split(inverse)
    right = jnp.concatenate([high, middle, high], axis=1)
    load.wait()
    rows = ROWS_DEV // OUT_CHUNKS
    stores = []
    for i in range(OUT_CHUNKS):
        part = pl.ds(i * rows, rows)
        high, middle, _ = split(summed[part, :])
        ortho[part, :] = lax.dot_general(
            jnp.concatenate([high, high, middle], axis=1),
            right,
            (((1,), (1,)), ((), ())),
            preferred_element_type=jnp.float32,
        )
        store = pltpu.make_async_copy(ortho.at[part, :], ortho_hbm.at[part, :], out_sems.at[i])
        store.start()
        stores.append(store)
    for store in stores:
        store.wait()


def finish(me, mine, other, summed):
    return pl.pallas_call(
        finish_kernel,
        out_shape=(
            jax.ShapeDtypeStruct((ROWS_DEV, BASIS), jnp.float32),
            jax.ShapeDtypeStruct((BASIS, BASIS), jnp.float32),
        ),
        in_specs=[
            pl.BlockSpec(memory_space=pltpu.SMEM),
            pl.BlockSpec(memory_space=pltpu.VMEM),
            pl.BlockSpec(memory_space=pltpu.VMEM),
            pl.BlockSpec(memory_space=pl.ANY),
        ],
        out_specs=(pl.BlockSpec(memory_space=pl.ANY), pl.BlockSpec(memory_space=pltpu.VMEM)),
        scratch_shapes=[
            pltpu.VMEM((3 * BLOCK, BLOCK), jnp.float32),
            pltpu.VMEM((BASIS, 2 * BASIS), jnp.float32),
            pltpu.VMEM((ROWS_DEV, BASIS), jnp.float32),
            pltpu.VMEM((ROWS_DEV, BASIS), jnp.float32),
            pltpu.SemaphoreType.DMA,
            pltpu.SemaphoreType.DMA((OUT_CHUNKS,)),
        ],
        compiler_params=pltpu.CompilerParams(vmem_limit_bytes=40 * 1024 * 1024),
        name="finish",
    )(me, mine, other, summed)


def local(tiles, tile_src, tile_out, basis0):
    row = lax.axis_index("row").astype(jnp.int32)
    col = lax.axis_index("col").astype(jnp.int32)
    me = jnp.stack([col & 1, (col >> 1) & 3])
    src = tile_src[0, 0]
    group = src >> 4
    distance = (((group >> 1) - (row >> 1)) & 3) + 4 * ((group + row) & 1)
    src = distance * BLOCKS_DEV + (src & 15)

    parts, place = gather_column(basis0, tile_out[0, 0] & 15)
    products = make_products(src, tiles[0, 0], parts)
    products, place, me = together(products, place, me)
    products = lax.all_to_all(
        products.reshape(N_COL, PER_PEER * BLOCK, BASIS), "col", 0, 0, tiled=True
    )
    summed, gram = sum_and_gram(place, me, products.reshape(-1, BASIS))
    return finish(me, *reduce_everywhere(gram), summed)


def solution(mesh):
    in_specs = (
        P("row", "col", None, None, None),
        P("row", "col", None),
        P("row", "col", None),
        P(("row", "col"), None),
    )
    out_specs = (P(("row", "col"), None), P())
    return jax.shard_map(local, mesh=mesh, in_specs=in_specs, out_specs=out_specs, check_vma=False)
```
